32 devices in a mesh: layer: 16 (over z, y, x), dp: 2 (over core).
Axes of the slice: x: 2, y: 2, z: 4, core: 2. Of those that a mesh axis runs over, the one named last changes fastest.
Arguments:
- states: float32 [16, 2, 24, 1536], P('layer', 'dp'), may hold values from -6 to 6
- adjoints: float32 [16, 2, 24, 1536], P('layer', 'dp'), may hold values from -6 to 6
- kernels: bfloat16 [64, 3, 3, 64, 64], P('layer'), may hold values from -0.25 to 0.25
- biases: float32 [64, 64], P('layer'), may hold values from -4 to 4
- coarse_gain: float32 [16, 64], P('layer'), may hold values from 0.01 to 1
Outputs:
- states_new: float32 [16, 2, 24, 1536], P('layer', 'dp')
- adjoints_new: float32 [16, 2, 24, 1536], P('layer', 'dp')
- kernel_grad: float32 [64, 3, 3, 64, 64], P('layer')
- bias_grad: float32 [64, 64], P('layer')
The draws below stay inside these ranges and needn't reach their ends.
All inputs are finite; a program needn't handle non-finite values.
Results may differ from the reference program's by a relative error of at most 0.0054.
Values sent between devices are 32-bit elements; how exact they have to be, the bound alone decides.
A program may use at most 64 MiB of HBM per device.

```python
import jax
import jax.numpy as jnp
from jax import lax

CH = 64
HEIGHT = 24
WIDTH = 24
LPD = 4
NBLOCKS = 16
LAYERS = 64
IMAGES = 2


def draw_coarse_gain(key, part):
    subkeys = jax.random.split(key, 6)
    portion = 0.5
    lasting = jax.random.uniform(subkeys[0], (CH,)) < portion
    extent = jax.random.uniform(subkeys[1], (CH,), minval=0.2, maxval=1.0)
    spread = jnp.exp(jax.random.uniform(subkeys[2], (NBLOCKS, CH), minval=-0.7, maxval=0.7))
    slow_gain = jnp.exp(-extent[None, :] * spread / NBLOCKS)
    positions = jax.random.randint(subkeys[3], (2,), 0, NBLOCKS)
    struck = jnp.any(jnp.arange(NBLOCKS)[:, None] == positions[None, :], axis=1)
    factor = jax.random.uniform(subkeys[4], (NBLOCKS, CH), minval=0.6, maxval=0.8)
    slow_gain = jnp.where(struck[:, None], slow_gain * factor, slow_gain)
    fast_gain = jnp.exp(-jax.random.uniform(subkeys[5], (NBLOCKS, CH), minval=1.0, maxval=3.0))
    return jnp.where(lasting[None, :], slow_gain, fast_gain).astype(jnp.float32)


def block_levels(key, shape, cuts, smallest, largest):
    def one(axis_at, blocks):
        heights = jax.random.uniform(jax.random.fold_in(jax.random.fold_in(key, 6), axis_at), (blocks,), jnp.float32, smallest / len(cuts), largest / len(cuts))
        return jnp.repeat(jnp.exp(heights), shape[axis_at] // blocks).reshape((-1,) + (1,) * (len(shape) - axis_at - 1))

    loudness = one(*cuts[0])
    for cut in cuts[1:]:
        loudness = loudness * one(*cut)
    return loudness


def centred(key, shape, scale, most, shards=(), dtype=jnp.bfloat16):
    loudness = block_levels(key, shape, shards, -0.22, 0.18) if shards else 1.0
    values = jax.random.normal(key, shape, jnp.float32) * scale * loudness
    return jnp.minimum(jnp.maximum(values, -most), most).astype(dtype)


def setup_inputs(seed: int = 0) -> dict:
    key_of = jax.random.split(jax.random.key(seed), 6)
    return {
        "states": centred(key_of[0], (NBLOCKS, IMAGES, HEIGHT, WIDTH * CH), 1.0, 6.0, ((0, 16), (1, 2)), jnp.float32),
        "adjoints": centred(key_of[1], (NBLOCKS, IMAGES, HEIGHT, WIDTH * CH), 1.0, 6.0, ((0, 16), (1, 2)), jnp.float32),
        "kernels": centred(key_of[2], (LAYERS, 3, 3, CH, CH), (9 * CH) ** -0.5, 0.25, ((0, 16),)),
        "biases": centred(key_of[3], (LAYERS, CH), 1.0, 4.0, ((0, 16),), jnp.float32),
        "coarse_gain": draw_coarse_gain(jax.random.fold_in(key_of[5], 71), 0),
    }


step_size = 0.5


def correlate(field, kernel):
    return lax.conv_general_dilated(field, kernel, (1, 1), "SAME", dimension_numbers=("NHWC", "HWIO", "NHWC"), precision=lax.Precision.HIGHEST)


def rounded(values):
    return values.astype(jnp.bfloat16).astype(jnp.float32)


def activation(field, kernel, bias):
    return jnp.tanh(correlate(rounded(field), kernel.astype(jnp.float32)) + bias)


def kernel_terms(field, sens_round):
    rows_img = field.shape[1]
    cols_img = field.shape[2]
    channels = field.shape[3]
    padded = jnp.pad(rounded(field), ((0, 0), (1, 1), (1, 1), (0, 0)))
    patches = jnp.stack([padded[:, row:row + rows_img, col:col + cols_img] for row in range(3) for col in range(3)])
    summed = jnp.einsum("knhwi,nhwo->kio", patches, sens_round, precision=lax.Precision.HIGHEST)
    return summed.reshape(3, 3, channels, channels)


def block_pass(start, finish_adjoint, kernels, biases):
    field = start
    path = []
    acts = []
    depth_count = kernels.shape[0]
    for depth in range(depth_count):
        activ = activation(field, kernels[depth], biases[depth])
        path.append(field)
        acts.append(activ)
        field = field + step_size * activ
    adjoint = finish_adjoint
    kgrads = [None] * depth_count
    bgrads = [None] * depth_count
    for depth in reversed(range(depth_count)):
        sens = step_size * (1.0 - acts[depth] * acts[depth]) * adjoint
        sens_round = rounded(sens)
        flipped = kernels[depth][::-1, ::-1].transpose(0, 1, 3, 2).astype(jnp.float32)
        adjoint = adjoint + correlate(sens_round, flipped)
        kgrads[depth] = kernel_terms(path[depth], sens_round)
        bgrads[depth] = jnp.sum(sens, axis=(0, 1, 2))
    return field, adjoint, jnp.stack(kgrads), jnp.stack(bgrads)


def reference(states, adjoints, kernels, biases, coarse_gain):
    block_count, count_img, rows_img, flat = states.shape
    channels = kernels.shape[-1]
    cols_img = flat // channels
    shape_four = (count_img, rows_img, cols_img, channels)
    grouped_kernels = kernels.reshape(block_count, LPD, 3, 3, channels, channels)
    grouped_biases = biases.reshape(block_count, LPD, channels)

    def visit(carry, inputs):
        start, finish_adj, kern, bias = inputs
        finish, begin_adj, kgrad, bgrad = block_pass(start.reshape(shape_four), finish_adj.reshape(shape_four), kern, bias)
        return carry, (finish.reshape(count_img, rows_img, flat), begin_adj.reshape(count_img, rows_img, flat), kgrad, bgrad)

    _, (finish, begin_adj, kgrad, bgrad) = lax.scan(visit, jnp.zeros((), jnp.float32), (states, adjoints, grouped_kernels, grouped_biases))
    gain_rows = jnp.tile(coarse_gain, (1, cols_img)).reshape(block_count, 1, 1, flat)

    def forward_step(current, inputs):
        gain, older, finish_now = inputs
        following = gain * (current - older) + finish_now
        return following, following

    _, later = lax.scan(forward_step, states[0], (gain_rows[:-1], states[:-1], finish[:-1]))
    states_new = jnp.concatenate([states[:1], later], axis=0)

    def backward_step(current, inputs):
        gain, guess, begin_now = inputs
        earlier = gain * (current - guess) + begin_now
        return earlier, earlier

    _, before = lax.scan(backward_step, begin_adj[-1], (gain_rows[:-1], adjoints[:-1], begin_adj[:-1]), reverse=True)
    adjoints_new = jnp.concatenate([before, begin_adj[-1:]], axis=0)
    kernel_grad = kgrad.reshape(block_count * LPD, 3, 3, channels, channels) / count_img
    bias_grad = bgrad.reshape(block_count * LPD, channels) / count_img
    return states_new, adjoints_new, kernel_grad, bias_grad
```

```python
import functools

import jax
import jax.numpy as jnp
from jax import lax
from jax.experimental import pallas as pl
from jax.experimental.pallas import tpu as pltpu
from jax.sharding import PartitionSpec as P

step_size = 0.5
MESH = pl.DeviceIdType.MESH
F32 = jnp.float32
BF16 = jnp.bfloat16


def down(array, count):
    zero = jnp.zeros((count, array.shape[1]), array.dtype)
    return jnp.concatenate([zero, array[:-count]], axis=0)


def up(array, count):
    zero = jnp.zeros((count, array.shape[1]), array.dtype)
    return jnp.concatenate([array[count:], zero], axis=0)


def pack(array):
    half = array.shape[0] // 2
    return jnp.concatenate([array[:half], array[half:]], axis=1)


def kernel(
    n, m, c, owners, cols, images,
    st, adj, ker, bias, gain,
    out_s, out_a, out_k, out_b,
    xs, acts, s3s, kf, fsend, asend, fin, ain, fout, aout, fres, ares, gbuf,
    fs_send, fs_recv, as_send, as_recv, fr_send, fr_recv, ar_send, ar_recv, g_send, g_recv,
):
    me = lax.axis_index("layer")
    mine = lax.axis_index("dp")
    depth_count = ker.shape[0]
    ch = ker.shape[-1]
    cells = st.shape[0]
    half = cells // 2

    barrier = pltpu.get_barrier_semaphore()

    def greet(k, carry):
        pl.semaphore_signal(
            barrier, inc=1, device_id={"layer": lax.rem(me + k, n)}, device_id_type=MESH
        )
        return carry

    def greet_dp(k, carry):
        pl.semaphore_signal(
            barrier, inc=1, device_id={"dp": lax.rem(mine + k, m)}, device_id_type=MESH
        )
        return carry

    lax.fori_loop(1, n, greet, 0)
    lax.fori_loop(1, m, greet_dp, 0)

    column = lax.rem(lax.broadcasted_iota(jnp.int32, (cells, ch), 0), cols)
    has_left = column > 0
    has_right = column < cols - 1

    for d in range(depth_count):
        kf[d] = jnp.concatenate(
            [
                jnp.concatenate([ker[d, dy, dx] for dx in range(3)], axis=0)
                for dy in range(3)
            ],
            axis=1,
        )

    field = st[...]
    for d in range(depth_count):
        left = jnp.where(has_left, down(field, 1), 0.0)
        right = jnp.where(has_right, up(field, 1), 0.0)
        x = jnp.concatenate([left, field, right], axis=1).astype(BF16)
        xs[d] = x
        y = jnp.dot(x, kf[d], preferred_element_type=F32)
        total = down(y[:, :ch], cols) + y[:, ch : 2 * ch] + up(y[:, 2 * ch :], cols)
        act = jnp.tanh(total + bias[d : d + 1, :])
        acts[d] = act
        field = field + step_size * act

    gain_row = gain[...]
    zero_row = jnp.zeros_like(gain_row)
    lead = jnp.where(me == 0, zero_row, gain_row)
    tail = jnp.where(me == n - 1, zero_row, gain_row)
    gain_two = jnp.concatenate([gain_row, gain_row], axis=1)

    pl.semaphore_wait(barrier, n - 1 + m - 1)

    def scatter(src, dst, send, recv, peer):
        return pltpu.make_async_remote_copy(
            src_ref=src.at[peer], dst_ref=dst.at[me],
            send_sem=send.at[peer], recv_sem=recv.at[me],
            device_id={"layer": peer}, device_id_type=MESH,
        )

    def arrived(dst, send, recv, source):
        pltpu.make_async_remote_copy(
            src_ref=dst.at[source], dst_ref=dst.at[source],
            send_sem=send.at[source], recv_sem=recv.at[source],
            device_id={"layer": source}, device_id_type=MESH,
        ).wait_recv()

    def scatter_all(src, dst, send, recv):
        def go(k, carry):
            peer = lax.rem(me + k, n)

            @pl.when(peer < owners)
            def _():
                scatter(src, dst, send, recv, peer).start()

            return carry

        lax.fori_loop(1, n, go, 0)

    def scatter_sent(src, dst, send, recv):
        def go(k, carry):
            peer = lax.rem(me + k, n)

            @pl.when(peer < owners)
            def _():
                scatter(src, dst, send, recv, peer).wait_send()

            return carry

        lax.fori_loop(1, n, go, 0)

    def arrived_all(dst, send, recv):
        def go(k, carry):
            arrived(dst, send, recv, lax.rem(me + k, n))
            return carry

        lax.fori_loop(1, n, go, 0)

    def give_all(src, dst, send, recv):
        def go(k, carry):
            scatter(src, dst, send, recv, lax.rem(me + k, n)).start()
            return carry

        lax.fori_loop(1, n, go, 0)

    def given_all(src, dst, send, recv):
        def go(k, carry):
            scatter(src, dst, send, recv, lax.rem(me + k, n)).wait_send()
            return carry

        lax.fori_loop(1, n, go, 0)

    def taken_all(dst, send, recv):
        def go(k, carry):
            source = lax.rem(me + k, n)

            @pl.when(source < owners)
            def _():
                arrived(dst, send, recv, source)

            return carry

        lax.fori_loop(1, n, go, 0)

    fsend[:, :c] = pack(field - lead * st[...]).reshape(owners, c, 2 * ch)
    fsend[:, c:] = jnp.broadcast_to(gain_two[None], (owners, 8, 2 * ch))
    scatter_all(fsend, fin, fs_send, fs_recv)

    lam = adj[...]
    for d in reversed(range(depth_count)):
        act = acts[d]
        sens = step_size * (1.0 - act * act) * lam
        total = jnp.sum(sens, axis=0, keepdims=True)
        gbuf[mine, d, 3 * ch :, :] = jnp.broadcast_to(
            jnp.concatenate([total, total, total], axis=1), (8, 3 * ch)
        )
        s3 = jnp.concatenate([up(sens, cols), sens, down(sens, cols)], axis=1).astype(BF16)
        s3s[d] = s3
        t = lax.dot_general(s3, kf[d], (((1,), (1,)), ((), ())), preferred_element_type=F32)
        lam = (
            lam
            + t[:, ch : 2 * ch]
            + jnp.where(has_right, up(t[:, :ch], 1), 0.0)
            + jnp.where(has_left, down(t[:, 2 * ch :], 1), 0.0)
        )

    asend[...] = pack(lam - tail * adj[...]).reshape(owners, c, 2 * ch)
    scatter_all(asend, ain, as_send, as_recv)

    @pl.when(me < owners)
    def _():
        fin[me] = fsend[me]
        ain[me] = asend[me]
        arrived_all(fin, fs_send, fs_recv)

        def turn(k, run):
            fout[k] = run
            part = fin[k]
            return part[c : c + 1] * run + part[:c]

        lax.fori_loop(0, n, turn, jnp.zeros((c, 2 * ch), F32))
        fres[me] = fout[me]
        give_all(fout, fres, fr_send, fr_recv)

    def pair(d, peer):
        return pltpu.make_async_remote_copy(
            src_ref=gbuf.at[mine, d], dst_ref=gbuf.at[mine, d],
            send_sem=g_send.at[peer, d], recv_sem=g_recv.at[mine, d],
            device_id={"dp": peer}, device_id_type=MESH,
        )

    def share(d):
        gbuf[mine, d, : 3 * ch, :] = lax.dot_general(
            xs[d], s3s[d], (((0,), (0,)), ((), ())), preferred_element_type=F32
        )

        def go(k, carry):
            pair(d, lax.rem(mine + k, m)).start()
            return carry

        lax.fori_loop(1, m, go, 0)

    for d in range(depth_count // 2):
        share(d)

    @pl.when(me < owners)
    def _():
        arrived_all(ain, as_send, as_recv)

        def turn(k, run):
            at = n - 1 - k
            new = fin[at, c : c + 1, :] * run + ain[at]
            aout[at] = new
            return new

        lax.fori_loop(0, n, turn, jnp.zeros((c, 2 * ch), F32))
        ares[me] = aout[me]
        give_all(aout, ares, ar_send, ar_recv)

    for d in range(depth_count // 2, depth_count):
        share(d)

    taken_all(fres, fr_send, fr_recv)
    new = fres[...].reshape(half, 2 * ch)

    @pl.when(me == 0)
    def _():
        out_s[...] = st[...]

    @pl.when(me > 0)
    def _():
        out_s[:half] = new[:, :ch]
        out_s[half:] = new[:, ch:]

    for d in range(depth_count):

        def go(k, carry):
            source = lax.rem(mine + k, m)
            pltpu.make_async_remote_copy(
                src_ref=gbuf.at[source, d], dst_ref=gbuf.at[source, d],
                send_sem=g_send.at[source, d], recv_sem=g_recv.at[source, d],
                device_id={"dp": source}, device_id_type=MESH,
            ).wait_recv()
            return carry

        lax.fori_loop(1, m, go, 0)
        total = gbuf[0, d]
        for k in range(1, m):
            total = total + gbuf[k, d]
        total = total * (1.0 / images)
        for dy in range(3):
            for dx in range(3):
                out_k[d, dy, dx] = total[dx * ch : (dx + 1) * ch, dy * ch : (dy + 1) * ch]
        out_b[d : d + 1, :] = total[3 * ch : 3 * ch + 1, :ch]

    taken_all(ares, ar_send, ar_recv)
    new = ares[...].reshape(half, 2 * ch)
    out_a[:half] = new[:, :ch]
    out_a[half:] = new[:, ch:]

    scatter_sent(fsend, fin, fs_send, fs_recv)
    scatter_sent(asend, ain, as_send, as_recv)

    @pl.when(me < owners)
    def _():
        given_all(fout, fres, fr_send, fr_recv)
        given_all(aout, ares, ar_send, ar_recv)

    for d in range(depth_count):

        def gone(k, carry):
            pair(d, lax.rem(mine + k, m)).wait_send()
            return carry

        lax.fori_loop(1, m, gone, 0)


def body(states, adjoints, kernels, biases, coarse_gain):
    rows, flat = states.shape[2], states.shape[3]
    depth_count, ch = kernels.shape[0], kernels.shape[-1]
    cols = flat // ch
    cells = rows * cols
    half = cells // 2
    n, m = lax.axis_size("layer"), lax.axis_size("dp")
    images = m * states.shape[1]
    c = next(k for k in range(8, half + 1, 8) if half % k == 0 and half // k <= n)
    owners = half // c
    vmem = pl.BlockSpec(memory_space=pltpu.VMEM)
    wide = 2 * ch
    dma = pltpu.SemaphoreType.DMA
    new_s, new_a, kgrad, bgrad = pl.pallas_call(
        functools.partial(kernel, n, m, c, owners, cols, images),
        out_shape=(
            jax.ShapeDtypeStruct((cells, ch), F32),
            jax.ShapeDtypeStruct((cells, ch), F32),
            jax.ShapeDtypeStruct(kernels.shape, F32),
            jax.ShapeDtypeStruct(biases.shape, F32),
        ),
        in_specs=[vmem] * 5,
        out_specs=(vmem,) * 4,
        scratch_shapes=[
            pltpu.VMEM((depth_count, cells, 3 * ch), BF16),
            pltpu.VMEM((depth_count, cells, ch), F32),
            pltpu.VMEM((depth_count, cells, 3 * ch), BF16),
            pltpu.VMEM((depth_count, 3 * ch, 3 * ch), BF16),
            pltpu.VMEM((owners, c + 8, wide), F32),
            pltpu.VMEM((owners, c, wide), F32),
            pltpu.VMEM((n, c + 8, wide), F32),
            pltpu.VMEM((n, c, wide), F32),
            pltpu.VMEM((n, c, wide), F32),
            pltpu.VMEM((n, c, wide), F32),
            pltpu.VMEM((owners, c, wide), F32),
            pltpu.VMEM((owners, c, wide), F32),
            pltpu.VMEM((m, depth_count, 3 * ch + 8, 3 * ch), F32),
        ]
        + [dma((n,))] * 8
        + [dma((m, depth_count))] * 2,
        compiler_params=pltpu.CompilerParams(
            collective_id=0, has_side_effects=True, vmem_limit_bytes=48 * 1024 * 1024
        ),
    )(
        states.reshape(cells, ch),
        adjoints.reshape(cells, ch),
        kernels,
        biases,
        coarse_gain,
    )
    return (
        new_s.reshape(states.shape),
        new_a.reshape(states.shape),
        kgrad,
        bgrad,
    )


def solution(mesh):
    return jax.shard_map(
        body,
        mesh=mesh,
        in_specs=(
            P("layer", "dp", None, None),
            P("layer", "dp", None, None),
            P("layer", None, None, None, None),
            P("layer", None),
            P("layer", None),
        ),
        out_specs=(
            P("layer", "dp", None, None),
            P("layer", "dp", None, None),
            P("layer", None, None, None, None),
            P("layer", None),
        ),
        check_vma=False,
    )
```

```python
import functools

import jax
import jax.numpy as jnp
from jax import lax
from jax.experimental import pallas as pl
from jax.experimental.pallas import tpu as pltpu
from jax.sharding import PartitionSpec as P

step_size = 0.5
group = 4
MESH = pl.DeviceIdType.MESH
F32 = jnp.float32
BF16 = jnp.bfloat16


def down(array, count):
    zero = jnp.zeros((count, array.shape[1]), array.dtype)
    return jnp.concatenate([zero, array[:-count]], axis=0)


def up(array, count):
    zero = jnp.zeros((count, array.shape[1]), array.dtype)
    return jnp.concatenate([array[count:], zero], axis=0)


def cells_of(array, rows, ch):
    count = array.shape[1] // ch
    return jnp.concatenate([array[:, k * ch : (k + 1) * ch] for k in range(count)], axis=0)


def pack(array, rows, dst):
    share = array.shape[0] // (2 * rows * group)
    for k in range(group * share):
        at = 2 * k * rows
        to = (k % share) * rows
        dst[k // share, to : to + rows] = jnp.concatenate(
            [array[at : at + rows], array[at + rows : at + 2 * rows]], axis=1
        )


def unpack(src, dst, rows):
    share = src.shape[1] // rows
    wide = src.shape[2]
    for k in range(group * share):
        at = (k % share) * rows
        dst[:, k * wide : (k + 1) * wide] = src[k // share, at : at + rows]


def store(out_s, out_a, out_k, out_b, to_s, to_a, to_k, to_b, sems):
    copies = [
        pltpu.make_async_copy(src, dst, sems.at[k])
        for k, (src, dst) in enumerate(
            [(out_k, to_k), (out_s, to_s.at[0, 0]), (out_a, to_a.at[0, 0]), (out_b, to_b)]
        )
    ]
    for copy in copies:
        copy.start()
    for copy in copies:
        copy.wait()


def kernel(
    n, m, c, images,
    st_any, adj_any, ker_any, bias_any, gain_any,
    out_s, out_a, out_k, out_b,
    st, adj, ker, bias, gain, in_sem,
    xs, acts, s3s, kf, fsend, asend, fin, ain, fcomp, acomp, fz, az, fout, aout, fres, ares, gbuf,
    fs_send, fs_recv, as_send, as_recv, fr_send, fr_recv, ar_send, ar_recv,
    fz_send, fz_recv, az_send, az_recv, g_send, g_recv,
):
    me = lax.axis_index("layer")
    mine = lax.axis_index("dp")
    depth_count = ker.shape[0]
    ch = ker.shape[-1]
    flat = st.shape[1]
    cells = c * flat // ch
    top = asend.shape[1]

    loads = [
        pltpu.make_async_copy(src, dst, in_sem.at[k])
        for k, (src, dst) in enumerate(
            [
                (ker_any, ker),
                (st_any.at[0, 0], st),
                (bias_any, bias),
                (adj_any.at[0, 0], adj),
                (gain_any, gain),
            ]
        )
    ]
    for load in loads:
        load.start()

    barrier = pltpu.get_barrier_semaphore()

    place = lax.rem(me, group)
    plane = me // group
    planes = n // group

    def signal(target):
        pl.semaphore_signal(barrier, inc=1, device_id=target, device_id_type=MESH)

    def greet(k, carry):
        signal({"layer": lax.rem(plane + k, planes) * group + place})
        return carry

    def greet_dp(k, carry):
        signal({"dp": lax.rem(mine + k, m)})
        return carry

    for k in range(1, group):
        signal({"layer": plane * group + lax.rem(place + k, group)})
    lax.fori_loop(1, planes, greet, 0)
    lax.fori_loop(1, m, greet_dp, 0)

    row = lax.rem(lax.broadcasted_iota(jnp.int32, (cells, ch), 0), c)
    has_left = row > 0
    has_right = row < c - 1
    loads[0].wait()

    for d in range(depth_count):
        kf[d] = jnp.concatenate(
            [
                jnp.concatenate([ker[d, dy, dx] for dy in range(3)], axis=0)
                for dx in range(3)
            ],
            axis=1,
        )

    loads[1].wait()
    start = cells_of(st[...], c, ch)
    field = start
    loads[2].wait()
    for d in range(depth_count):
        left = jnp.where(has_left, down(field, 1), 0.0)
        right = jnp.where(has_right, up(field, 1), 0.0)
        x = jnp.concatenate([left, field, right], axis=1).astype(BF16)
        xs[d] = x
        y = jnp.dot(x, kf[d], preferred_element_type=F32)
        total = down(y[:, :ch], c) + y[:, ch : 2 * ch] + up(y[:, 2 * ch :], c)
        act = jnp.tanh(total + bias[d : d + 1, :])
        acts[d] = act
        field = field + step_size * act

    loads[3].wait()
    loads[4].wait()
    gain_row = gain[...]
    zero_row = jnp.zeros_like(gain_row)
    lead = jnp.where(me == 0, zero_row, gain_row)
    tail = jnp.where(me == n - 1, zero_row, gain_row)
    gain_two = jnp.concatenate([gain_row, gain_row], axis=1)

    pl.semaphore_wait(barrier, group - 1 + planes - 1 + m - 1)

    def across(src, dst, send, recv, k):
        peer = lax.rem(place + k, group)
        return pltpu.make_async_remote_copy(
            src_ref=src.at[peer], dst_ref=dst.at[place],
            send_sem=send.at[peer], recv_sem=recv.at[place],
            device_id={"layer": plane * group + peer}, device_id_type=MESH,
        )

    def along(src, dst, send, recv, to):
        return pltpu.make_async_remote_copy(
            src_ref=src, dst_ref=dst.at[plane],
            send_sem=send.at[to], recv_sem=recv.at[plane],
            device_id={"layer": to * group + place}, device_id_type=MESH,
        )

    def arrived(dst, send, recv, slot, source):
        pltpu.make_async_remote_copy(
            src_ref=dst.at[slot], dst_ref=dst.at[slot],
            send_sem=send.at[slot], recv_sem=recv.at[slot],
            device_id={"layer": source}, device_id_type=MESH,
        ).wait_recv()

    def scatter_all(*refs):
        for k in range(1, group):
            across(*refs, k).start()

    def scatter_sent(*refs):
        for k in range(1, group):
            across(*refs, k).wait_send()

    def arrived_all(dst, send, recv):
        for k in range(1, group):
            slot = lax.rem(place + k, group)
            arrived(dst, send, recv, slot, plane * group + slot)

    def along_all(low, high, *refs):
        def go(to, carry):
            along(*refs, to).start()
            return carry

        lax.fori_loop(low, high, go, 0)

    def along_sent(low, high, *refs):
        def go(to, carry):
            along(*refs, to).wait_send()
            return carry

        lax.fori_loop(low, high, go, 0)

    def compose(parts, comp, order):
        run = parts[order[0], :top]
        all_gain = fin[order[0], top : top + 1]
        for k in order[1:]:
            step = fin[k, top : top + 1]
            run = step * run + parts[k, :top]
            all_gain = step * all_gain
        comp[:top] = run
        comp[top:] = jnp.broadcast_to(all_gain, (8, 2 * ch))

    pack(field - lead * start, c, fsend)
    fsend[:, top:] = jnp.broadcast_to(gain_two[None], (group, 8, 2 * ch))
    scatter_all(fsend, fin, fs_send, fs_recv)

    end = cells_of(adj[...], c, ch)
    lam = end
    for d in reversed(range(depth_count)):
        act = acts[d]
        sens = step_size * (1.0 - act * act) * lam
        total = jnp.sum(sens, axis=0, keepdims=True)
        gbuf[mine, d, 3 * ch :, :] = jnp.broadcast_to(
            jnp.concatenate([total, total, total], axis=1), (8, 3 * ch)
        )
        s3 = jnp.concatenate([up(sens, c), sens, down(sens, c)], axis=1).astype(BF16)
        s3s[d] = s3
        t = lax.dot_general(s3, kf[d], (((1,), (1,)), ((), ())), preferred_element_type=F32)
        lam = (
            lam
            + t[:, ch : 2 * ch]
            + jnp.where(has_right, up(t[:, :ch], 1), 0.0)
            + jnp.where(has_left, down(t[:, 2 * ch :], 1), 0.0)
        )

    pack(lam - tail * end, c, asend)
    scatter_all(asend, ain, as_send, as_recv)

    fin[place] = fsend[place]
    ain[place] = asend[place]
    arrived_all(fin, fs_send, fs_recv)
    compose(fin, fcomp, range(group))
    along_all(plane + 1, planes, fcomp, fz, fz_send, fz_recv)
    arrived_all(ain, as_send, as_recv)
    compose(ain, acomp, range(group - 1, -1, -1))
    along_all(0, plane, acomp, az, az_send, az_recv)

    def pair(d, peer):
        return pltpu.make_async_remote_copy(
            src_ref=gbuf.at[mine, d], dst_ref=gbuf.at[mine, d],
            send_sem=g_send.at[peer, d], recv_sem=g_recv.at[mine, d],
            device_id={"dp": peer}, device_id_type=MESH,
        )

    def share(d):
        gbuf[mine, d, : 3 * ch, :] = lax.dot_general(
            xs[d], s3s[d], (((0,), (0,)), ((), ())), preferred_element_type=F32
        )

        def go(k, carry):
            pair(d, lax.rem(mine + k, m)).start()
            return carry

        lax.fori_loop(1, m, go, 0)

    for d in range(depth_count):
        share(d)

    def earlier(k, run):
        arrived(fz, fz_send, fz_recv, k, k * group + place)
        return fz[k, top : top + 1] * run + fz[k, :top]

    run = lax.fori_loop(0, plane, earlier, jnp.zeros((top, 2 * ch), F32))
    for k in range(group):
        fout[k] = run
        if k < group - 1:
            run = fin[k, top : top + 1] * run + fin[k, :top]
    fres[place] = fout[place]
    scatter_all(fout, fres, fr_send, fr_recv)

    def later(k, run):
        at = planes - 1 - k
        arrived(az, az_send, az_recv, at, at * group + place)
        return az[at, top : top + 1] * run + az[at, :top]

    run = lax.fori_loop(0, planes - 1 - plane, later, jnp.zeros((top, 2 * ch), F32))
    for k in range(group - 1, -1, -1):
        run = fin[k, top : top + 1] * run + ain[k]
        aout[k] = run
    ares[place] = aout[place]
    scatter_all(aout, ares, ar_send, ar_recv)

    arrived_all(fres, fr_send, fr_recv)

    @pl.when(me == 0)
    def _():
        out_s[...] = st[...]

    @pl.when(me > 0)
    def _():
        unpack(fres, out_s, c)

    for d in range(depth_count):

        def go(k, carry):
            source = lax.rem(mine + k, m)
            pltpu.make_async_remote_copy(
                src_ref=gbuf.at[source, d], dst_ref=gbuf.at[source, d],
                send_sem=g_send.at[source, d], recv_sem=g_recv.at[source, d],
                device_id={"dp": source}, device_id_type=MESH,
            ).wait_recv()
            return carry

        lax.fori_loop(1, m, go, 0)
        total = gbuf[0, d]
        for k in range(1, m):
            total = total + gbuf[k, d]
        total = total * (1.0 / images)
        for dy in range(3):
            for dx in range(3):
                out_k[d, dy, dx] = total[dy * ch : (dy + 1) * ch, dx * ch : (dx + 1) * ch]
        out_b[d : d + 1, :] = total[3 * ch : 3 * ch + 1, :ch]

    arrived_all(ares, ar_send, ar_recv)
    unpack(ares, out_a, c)

    scatter_sent(fsend, fin, fs_send, fs_recv)
    scatter_sent(asend, ain, as_send, as_recv)
    scatter_sent(fout, fres, fr_send, fr_recv)
    scatter_sent(aout, ares, ar_send, ar_recv)
    along_sent(plane + 1, planes, fcomp, fz, fz_send, fz_recv)
    along_sent(0, plane, acomp, az, az_send, az_recv)

    for d in range(depth_count):

        def gone(k, carry):
            pair(d, lax.rem(mine + k, m)).wait_send()
            return carry

        lax.fori_loop(1, m, gone, 0)


def body(states, adjoints, kernels, biases, coarse_gain):
    rows, flat = states.shape[2], states.shape[3]
    depth_count, ch = kernels.shape[0], kernels.shape[-1]
    cells = rows * flat // ch
    n, m = lax.axis_size("layer"), lax.axis_size("dp")
    images = m * states.shape[1]
    c = rows
    top = flat // (2 * ch) // group * rows
    planes = n // group
    vmem = pl.BlockSpec(memory_space=pltpu.VMEM)
    anywhere = pl.BlockSpec(memory_space=pl.ANY)
    hbm = pl.BlockSpec(memory_space=pltpu.HBM)
    wide = 2 * ch
    dma = pltpu.SemaphoreType.DMA
    results = pl.pallas_call(
        functools.partial(kernel, n, m, c, images),
        out_shape=(
            jax.ShapeDtypeStruct((rows, flat), F32),
            jax.ShapeDtypeStruct((rows, flat), F32),
            jax.ShapeDtypeStruct(kernels.shape, F32),
            jax.ShapeDtypeStruct(biases.shape, F32),
        ),
        in_specs=[hbm] * 5,
        out_specs=(vmem,) * 4,
        scratch_shapes=[
            pltpu.VMEM((rows, flat), F32),
            pltpu.VMEM((rows, flat), F32),
            pltpu.VMEM(kernels.shape, BF16),
            pltpu.VMEM(biases.shape, F32),
            pltpu.VMEM(coarse_gain.shape, F32),
            dma((5,)),
            pltpu.VMEM((depth_count, cells, 3 * ch), BF16),
            pltpu.VMEM((depth_count, cells, ch), F32),
            pltpu.VMEM((depth_count, cells, 3 * ch), BF16),
            pltpu.VMEM((depth_count, 3 * ch, 3 * ch), BF16),
            pltpu.VMEM((group, top + 8, wide), F32),
            pltpu.VMEM((group, top, wide), F32),
            pltpu.VMEM((group, top + 8, wide), F32),
            pltpu.VMEM((group, top, wide), F32),
            pltpu.VMEM((top + 8, wide), F32),
            pltpu.VMEM((top + 8, wide), F32),
            pltpu.VMEM((planes, top + 8, wide), F32),
            pltpu.VMEM((planes, top + 8, wide), F32),
            pltpu.VMEM((group, top, wide), F32),
            pltpu.VMEM((group, top, wide), F32),
            pltpu.VMEM((group, top, wide), F32),
            pltpu.VMEM((group, top, wide), F32),
            pltpu.VMEM((m, depth_count, 3 * ch + 8, 3 * ch), F32),
        ]
        + [dma((group,))] * 8
        + [dma((planes,))] * 4
        + [dma((m, depth_count))] * 2,
        compiler_params=pltpu.CompilerParams(
            collective_id=0, has_side_effects=True, vmem_limit_bytes=48 * 1024 * 1024
        ),
    )(states, adjoints, kernels, biases, coarse_gain)
    return pl.pallas_call(
        store,
        out_shape=(
            jax.ShapeDtypeStruct(states.shape, F32),
            jax.ShapeDtypeStruct(states.shape, F32),
            jax.ShapeDtypeStruct(kernels.shape, F32),
            jax.ShapeDtypeStruct(biases.shape, F32),
        ),
        in_specs=[anywhere] * 4,
        out_specs=(hbm,) * 4,
        scratch_shapes=[dma((4,))],
        compiler_params=pltpu.CompilerParams(vmem_limit_bytes=1024 * 1024),
    )(*results)


def solution(mesh):
    return jax.shard_map(
        body,
        mesh=mesh,
        in_specs=(
            P("layer", "dp", None, None),
            P("layer", "dp", None, None),
            P("layer", None, None, None, None),
            P("layer", None),
            P("layer", None),
        ),
        out_specs=(
            P("layer", "dp", None, None),
            P("layer", "dp", None, None),
            P("layer", None, None, None, None),
            P("layer", None),
        ),
        check_vma=False,
    )
```

```python
import functools

import jax
import jax.numpy as jnp
from jax import lax
from jax.experimental import pallas as pl
from jax.experimental.pallas import tpu as pltpu
from jax.sharding import PartitionSpec as P

step_size = 0.5
group = 4
MESH = pl.DeviceIdType.MESH
F32 = jnp.float32
BF16 = jnp.bfloat16


def down(array, count):
    zero = jnp.zeros((count, array.shape[1]), array.dtype)
    return jnp.concatenate([zero, array[:-count]], axis=0)


def up(array, count):
    zero = jnp.zeros((count, array.shape[1]), array.dtype)
    return jnp.concatenate([array[count:], zero], axis=0)


def cells_of(array, rows, ch):
    count = array.shape[1] // ch
    return jnp.concatenate([array[:, k * ch : (k + 1) * ch] for k in range(count)], axis=0)


def pack(array, rows, dst):
    share = array.shape[0] // (2 * rows * group)
    for k in range(group * share):
        at = 2 * k * rows
        to = (k % share) * rows
        dst[k // share, to : to + rows] = jnp.concatenate(
            [array[at : at + rows], array[at + rows : at + 2 * rows]], axis=1
        )


def unpack(src, dst, rows):
    share = src.shape[1] // rows
    wide = src.shape[2]
    for k in range(group * share):
        at = (k % share) * rows
        dst[:, k * wide : (k + 1) * wide] = src[k // share, at : at + rows]


def store(out_s, out_a, out_k, out_b, to_s, to_a, to_k, to_b, sems):
    copies = [
        pltpu.make_async_copy(src, dst, sems.at[k])
        for k, (src, dst) in enumerate(
            [(out_k, to_k), (out_s, to_s.at[0, 0]), (out_a, to_a.at[0, 0]), (out_b, to_b)]
        )
    ]
    for copy in copies:
        copy.start()
    for copy in copies:
        copy.wait()


def kernel(
    n, m, c, images,
    ends_any, ker_any, bias_any,
    out_s, out_a, out_k, out_b,
    st, adj, ker, bias, in_sem,
    xs, acts, s3s, kf, fsend, asend, fin, ain, fcomp, acomp, fz, az, fout, aout, fres, ares, gbuf,
    fs_send, fs_recv, as_send, as_recv, fr_send, fr_recv, ar_send, ar_recv,
    fz_send, fz_recv, az_send, az_recv, g_send, g_recv,
):
    me = lax.axis_index("layer")
    mine = lax.axis_index("dp")
    depth_count = ker.shape[0]
    ch = ker.shape[-1]
    flat = st.shape[1]
    cells = c * flat // ch
    top = asend.shape[1]

    loads = [
        pltpu.make_async_copy(src, dst, in_sem.at[k])
        for k, (src, dst) in enumerate(
            [
                (ker_any, ker),
                (ends_any.at[:c], st),
                (bias_any, bias),
                (ends_any.at[c:], adj),
            ]
        )
    ]
    for load in loads:
        load.start()

    barrier = pltpu.get_barrier_semaphore()

    place = lax.rem(me, group)
    plane = me // group
    planes = n // group

    def signal(target):
        pl.semaphore_signal(barrier, inc=1, device_id=target, device_id_type=MESH)

    def greet(k, carry):
        signal({"layer": lax.rem(plane + k, planes) * group + place})
        return carry

    def greet_dp(k, carry):
        signal({"dp": lax.rem(mine + k, m)})
        return carry

    for k in range(1, group):
        signal({"layer": plane * group + lax.rem(place + k, group)})
    lax.fori_loop(1, planes, greet, 0)
    lax.fori_loop(1, m, greet_dp, 0)

    row = lax.rem(lax.broadcasted_iota(jnp.int32, (cells, ch), 0), c)
    has_left = row > 0
    has_right = row < c - 1
    loads[0].wait()

    for d in range(depth_count):
        kf[d] = jnp.concatenate(
            [
                jnp.concatenate([ker[d, dy, dx] for dy in range(3)], axis=0)
                for dx in range(3)
            ],
            axis=1,
        )

    loads[1].wait()
    start = cells_of(st[...], c, ch)
    field = start
    loads[2].wait()
    for d in range(depth_count):
        left = jnp.where(has_left, down(field, 1), 0.0)
        right = jnp.where(has_right, up(field, 1), 0.0)
        x = jnp.concatenate([left, field, right], axis=1).astype(BF16)
        xs[d] = x
        y = jnp.dot(x, kf[d], preferred_element_type=F32)
        total = down(y[:, :ch], c) + y[:, ch : 2 * ch] + up(y[:, 2 * ch :], c)
        act = jnp.tanh(total + bias[d : d + 1, :])
        acts[d] = act
        field = field + step_size * act

    loads[3].wait()
    gain_row = bias[depth_count : depth_count + 1, :]
    zero_row = jnp.zeros_like(gain_row)
    lead = jnp.where(me == 0, zero_row, gain_row)
    tail = jnp.where(me == n - 1, zero_row, gain_row)
    gain_two = jnp.concatenate([gain_row, gain_row], axis=1)

    pl.semaphore_wait(barrier, group - 1 + planes - 1 + m - 1)

    def across(src, dst, send, recv, k):
        peer = lax.rem(place + k, group)
        return pltpu.make_async_remote_copy(
            src_ref=src.at[peer], dst_ref=dst.at[place],
            send_sem=send.at[peer], recv_sem=recv.at[place],
            device_id={"layer": plane * group + peer}, device_id_type=MESH,
        )

    def along(src, dst, send, recv, to):
        return pltpu.make_async_remote_copy(
            src_ref=src, dst_ref=dst.at[plane],
            send_sem=send.at[to], recv_sem=recv.at[plane],
            device_id={"layer": to * group + place}, device_id_type=MESH,
        )

    def arrived(dst, send, recv, slot, source):
        pltpu.make_async_remote_copy(
            src_ref=dst.at[slot], dst_ref=dst.at[slot],
            send_sem=send.at[slot], recv_sem=recv.at[slot],
            device_id={"layer": source}, device_id_type=MESH,
        ).wait_recv()

    def scatter_all(*refs):
        for k in range(1, group):
            across(*refs, k).start()

    def scatter_sent(*refs):
        for k in range(1, group):
            across(*refs, k).wait_send()

    def arrived_all(dst, send, recv):
        for k in range(1, group):
            slot = lax.rem(place + k, group)
            arrived(dst, send, recv, slot, plane * group + slot)

    def along_all(low, high, *refs):
        def go(to, carry):
            along(*refs, to).start()
            return carry

        lax.fori_loop(low, high, go, 0)

    def along_sent(low, high, *refs):
        def go(to, carry):
            along(*refs, to).wait_send()
            return carry

        lax.fori_loop(low, high, go, 0)

    def compose(parts, comp, order):
        run = parts[order[0], :top]
        all_gain = fin[order[0], top : top + 1]
        for k in order[1:]:
            step = fin[k, top : top + 1]
            run = step * run + parts[k, :top]
            all_gain = step * all_gain
        comp[:top] = run
        comp[top:] = jnp.broadcast_to(all_gain, (8, 2 * ch))

    pack(field - lead * start, c, fsend)
    fsend[:, top:] = jnp.broadcast_to(gain_two[None], (group, 8, 2 * ch))
    scatter_all(fsend, fin, fs_send, fs_recv)

    end = cells_of(adj[...], c, ch)
    lam = end
    for d in reversed(range(depth_count)):
        act = acts[d]
        sens = step_size * (1.0 - act * act) * lam
        total = jnp.sum(sens, axis=0, keepdims=True)
        gbuf[mine, d, 3 * ch :, :] = jnp.broadcast_to(
            jnp.concatenate([total, total, total], axis=1), (8, 3 * ch)
        )
        s3 = jnp.concatenate([up(sens, c), sens, down(sens, c)], axis=1).astype(BF16)
        s3s[d] = s3
        t = lax.dot_general(s3, kf[d], (((1,), (1,)), ((), ())), preferred_element_type=F32)
        lam = (
            lam
            + t[:, ch : 2 * ch]
            + jnp.where(has_right, up(t[:, :ch], 1), 0.0)
            + jnp.where(has_left, down(t[:, 2 * ch :], 1), 0.0)
        )

    pack(lam - tail * end, c, asend)
    scatter_all(asend, ain, as_send, as_recv)

    fin[place] = fsend[place]
    ain[place] = asend[place]
    arrived_all(fin, fs_send, fs_recv)
    compose(fin, fcomp, range(group))
    along_all(plane + 1, planes, fcomp, fz, fz_send, fz_recv)
    arrived_all(ain, as_send, as_recv)
    compose(ain, acomp, range(group - 1, -1, -1))
    along_all(0, plane, acomp, az, az_send, az_recv)

    def pair(d, peer):
        return pltpu.make_async_remote_copy(
            src_ref=gbuf.at[mine, d], dst_ref=gbuf.at[mine, d],
            send_sem=g_send.at[peer, d], recv_sem=g_recv.at[mine, d],
            device_id={"dp": peer}, device_id_type=MESH,
        )

    def share(d):
        gbuf[mine, d, : 3 * ch, :] = lax.dot_general(
            xs[d], s3s[d], (((0,), (0,)), ((), ())), preferred_element_type=F32
        )

        def go(k, carry):
            pair(d, lax.rem(mine + k, m)).start()
            return carry

        lax.fori_loop(1, m, go, 0)

    for d in range(depth_count):
        share(d)

    def earlier(k, run):
        arrived(fz, fz_send, fz_recv, k, k * group + place)
        return fz[k, top : top + 1] * run + fz[k, :top]

    run = lax.fori_loop(0, plane, earlier, jnp.zeros((top, 2 * ch), F32))
    for k in range(group):
        fout[k] = run
        if k < group - 1:
            run = fin[k, top : top + 1] * run + fin[k, :top]
    fres[place] = fout[place]
    scatter_all(fout, fres, fr_send, fr_recv)

    def later(k, run):
        at = planes - 1 - k
        arrived(az, az_send, az_recv, at, at * group + place)
        return az[at, top : top + 1] * run + az[at, :top]

    run = lax.fori_loop(0, planes - 1 - plane, later, jnp.zeros((top, 2 * ch), F32))
    for k in range(group - 1, -1, -1):
        run = fin[k, top : top + 1] * run + ain[k]
        aout[k] = run
    ares[place] = aout[place]
    scatter_all(aout, ares, ar_send, ar_recv)

    arrived_all(fres, fr_send, fr_recv)

    @pl.when(me == 0)
    def _():
        out_s[...] = st[...]

    @pl.when(me > 0)
    def _():
        unpack(fres, out_s, c)

    for d in range(depth_count):

        def go(k, carry):
            source = lax.rem(mine + k, m)
            pltpu.make_async_remote_copy(
                src_ref=gbuf.at[source, d], dst_ref=gbuf.at[source, d],
                send_sem=g_send.at[source, d], recv_sem=g_recv.at[source, d],
                device_id={"dp": source}, device_id_type=MESH,
            ).wait_recv()
            return carry

        lax.fori_loop(1, m, go, 0)
        total = gbuf[0, d]
        for k in range(1, m):
            total = total + gbuf[k, d]
        total = total * (1.0 / images)
        for dy in range(3):
            for dx in range(3):
                out_k[d, dy, dx] = total[dy * ch : (dy + 1) * ch, dx * ch : (dx + 1) * ch]
        out_b[d : d + 1, :] = total[3 * ch : 3 * ch + 1, :ch]

    arrived_all(ares, ar_send, ar_recv)
    unpack(ares, out_a, c)

    scatter_sent(fsend, fin, fs_send, fs_recv)
    scatter_sent(asend, ain, as_send, as_recv)
    scatter_sent(fout, fres, fr_send, fr_recv)
    scatter_sent(aout, ares, ar_send, ar_recv)
    along_sent(plane + 1, planes, fcomp, fz, fz_send, fz_recv)
    along_sent(0, plane, acomp, az, az_send, az_recv)

    for d in range(depth_count):

        def gone(k, carry):
            pair(d, lax.rem(mine + k, m)).wait_send()
            return carry

        lax.fori_loop(1, m, gone, 0)


def body(states, adjoints, kernels, biases, coarse_gain):
    rows, flat = states.shape[2], states.shape[3]
    depth_count, ch = kernels.shape[0], kernels.shape[-1]
    cells = rows * flat // ch
    n, m = lax.axis_size("layer"), lax.axis_size("dp")
    images = m * states.shape[1]
    c = rows
    top = flat // (2 * ch) // group * rows
    planes = n // group
    vmem = pl.BlockSpec(memory_space=pltpu.VMEM)
    anywhere = pl.BlockSpec(memory_space=pl.ANY)
    hbm = pl.BlockSpec(memory_space=pltpu.HBM)
    wide = 2 * ch
    dma = pltpu.SemaphoreType.DMA
    results = pl.pallas_call(
        functools.partial(kernel, n, m, c, images),
        out_shape=(
            jax.ShapeDtypeStruct((rows, flat), F32),
            jax.ShapeDtypeStruct((rows, flat), F32),
            jax.ShapeDtypeStruct(kernels.shape, F32),
            jax.ShapeDtypeStruct(biases.shape, F32),
        ),
        in_specs=[hbm] * 3,
        out_specs=(vmem,) * 4,
        scratch_shapes=[
            pltpu.VMEM((rows, flat), F32),
            pltpu.VMEM((rows, flat), F32),
            pltpu.VMEM(kernels.shape, BF16),
            pltpu.VMEM((depth_count + 1, ch), F32),
            dma((4,)),
            pltpu.VMEM((depth_count, cells, 3 * ch), BF16),
            pltpu.VMEM((depth_count, cells, ch), F32),
            pltpu.VMEM((depth_count, cells, 3 * ch), BF16),
            pltpu.VMEM((depth_count, 3 * ch, 3 * ch), BF16),
            pltpu.VMEM((group, top + 8, wide), F32),
            pltpu.VMEM((group, top, wide), F32),
            pltpu.VMEM((group, top + 8, wide), F32),
            pltpu.VMEM((group, top, wide), F32),
            pltpu.VMEM((top + 8, wide), F32),
            pltpu.VMEM((top + 8, wide), F32),
            pltpu.VMEM((planes, top + 8, wide), F32),
            pltpu.VMEM((planes, top + 8, wide), F32),
            pltpu.VMEM((group, top, wide), F32),
            pltpu.VMEM((group, top, wide), F32),
            pltpu.VMEM((group, top, wide), F32),
            pltpu.VMEM((group, top, wide), F32),
            pltpu.VMEM((m, depth_count, 3 * ch + 8, 3 * ch), F32),
        ]
        + [dma((group,))] * 8
        + [dma((planes,))] * 4
        + [dma((m, depth_count))] * 2,
        compiler_params=pltpu.CompilerParams(
            collective_id=0, has_side_effects=True, vmem_limit_bytes=48 * 1024 * 1024
        ),
    )(
        jnp.concatenate([states[0, 0], adjoints[0, 0]]),
        kernels,
        jnp.concatenate([biases, coarse_gain]),
    )
    return pl.pallas_call(
        store,
        out_shape=(
            jax.ShapeDtypeStruct(states.shape, F32),
            jax.ShapeDtypeStruct(states.shape, F32),
            jax.ShapeDtypeStruct(kernels.shape, F32),
            jax.ShapeDtypeStruct(biases.shape, F32),
        ),
        in_specs=[anywhere] * 4,
        out_specs=(hbm,) * 4,
        scratch_shapes=[dma((4,))],
        compiler_params=pltpu.CompilerParams(vmem_limit_bytes=1024 * 1024),
    )(*results)


def solution(mesh):
    return jax.shard_map(
        body,
        mesh=mesh,
        in_specs=(
            P("layer", "dp", None, None),
            P("layer", "dp", None, None),
            P("layer", None, None, None, None),
            P("layer", None),
            P("layer", None),
        ),
        out_specs=(
            P("layer", "dp", None, None),
            P("layer", "dp", None, None),
            P("layer", None, None, None, None),
            P("layer", None),
        ),
        check_vma=False,
    )
```

```python
import functools

import jax
import jax.numpy as jnp
from jax import lax
from jax.experimental import pallas as pl
from jax.experimental.pallas import tpu as pltpu
from jax.sharding import PartitionSpec as P

step_size = 0.5
group = 4
MESH = pl.DeviceIdType.MESH
F32 = jnp.float32
BF16 = jnp.bfloat16


def down(array, count):
    zero = jnp.zeros((count, array.shape[1]), array.dtype)
    return jnp.concatenate([zero, array[:-count]], axis=0)


def up(array, count):
    zero = jnp.zeros((count, array.shape[1]), array.dtype)
    return jnp.concatenate([array[count:], zero], axis=0)


def cells_of(array, rows, ch):
    count = array.shape[1] // ch
    return jnp.concatenate([array[:, k * ch : (k + 1) * ch] for k in range(count)], axis=0)


def pack(array, rows, dst):
    share = array.shape[0] // (2 * rows * group)
    for k in range(group * share):
        at = 2 * k * rows
        to = (k % share) * rows
        dst[k // share, to : to + rows] = jnp.concatenate(
            [array[at : at + rows], array[at + rows : at + 2 * rows]], axis=1
        )


def unpack(src, dst, rows):
    share = src.shape[1] // rows
    wide = src.shape[2]
    for k in range(group * share):
        at = (k % share) * rows
        dst[:, k * wide : (k + 1) * wide] = src[k // share, at : at + rows]


def store(out_s, out_a, out_k, out_b, to_s, to_a, to_k, to_b, sems):
    copies = [
        pltpu.make_async_copy(src, dst, sems.at[k])
        for k, (src, dst) in enumerate(
            [(out_k, to_k), (out_s, to_s.at[0, 0]), (out_a, to_a.at[0, 0]), (out_b, to_b)]
        )
    ]
    for copy in copies:
        copy.start()
    for copy in copies:
        copy.wait()


def kernel(
    n, m, c, images,
    ends, ker, bias,
    out_s, out_a, out_k, out_b,
    xs, acts, s3s, kf, fsend, asend, fin, ain, fcomp, acomp, fz, az, fout, aout, fres, ares, gbuf,
    fs_send, fs_recv, as_send, as_recv, fr_send, fr_recv, ar_send, ar_recv,
    fz_send, fz_recv, az_send, az_recv, g_send, g_recv,
):
    me = lax.axis_index("layer")
    mine = lax.axis_index("dp")
    depth_count = ker.shape[0]
    ch = ker.shape[-1]
    flat = ends.shape[1]
    st, adj = ends.at[:c], ends.at[c:]
    cells = c * flat // ch
    top = asend.shape[1]

    barrier = pltpu.get_barrier_semaphore()

    place = lax.rem(me, group)
    plane = me // group
    planes = n // group

    def signal(target):
        pl.semaphore_signal(barrier, inc=1, device_id=target, device_id_type=MESH)

    def greet(k, carry):
        signal({"layer": lax.rem(plane + k, planes) * group + place})
        return carry

    def greet_dp(k, carry):
        signal({"dp": lax.rem(mine + k, m)})
        return carry

    for k in range(1, group):
        signal({"layer": plane * group + lax.rem(place + k, group)})
    lax.fori_loop(1, planes, greet, 0)
    lax.fori_loop(1, m, greet_dp, 0)

    row = lax.rem(lax.broadcasted_iota(jnp.int32, (cells, ch), 0), c)
    has_left = row > 0
    has_right = row < c - 1

    for d in range(depth_count):
        kf[d] = jnp.concatenate(
            [
                jnp.concatenate([ker[d, dy, dx] for dy in range(3)], axis=0)
                for dx in range(3)
            ],
            axis=1,
        )

    start = cells_of(st[...], c, ch)
    field = start
    for d in range(depth_count):
        left = jnp.where(has_left, down(field, 1), 0.0)
        right = jnp.where(has_right, up(field, 1), 0.0)
        x = jnp.concatenate([left, field, right], axis=1).astype(BF16)
        xs[d] = x
        y = jnp.dot(x, kf[d], preferred_element_type=F32)
        total = down(y[:, :ch], c) + y[:, ch : 2 * ch] + up(y[:, 2 * ch :], c)
        act = jnp.tanh(total + bias[d : d + 1, :])
        acts[d] = act
        field = field + step_size * act

    gain_row = bias[depth_count : depth_count + 1, :]
    zero_row = jnp.zeros_like(gain_row)
    lead = jnp.where(me == 0, zero_row, gain_row)
    tail = jnp.where(me == n - 1, zero_row, gain_row)
    gain_two = jnp.concatenate([gain_row, gain_row], axis=1)

    pl.semaphore_wait(barrier, group - 1 + planes - 1 + m - 1)

    def across(src, dst, send, recv, k):
        peer = lax.rem(place + k, group)
        return pltpu.make_async_remote_copy(
            src_ref=src.at[peer], dst_ref=dst.at[place],
            send_sem=send.at[peer], recv_sem=recv.at[place],
            device_id={"layer": plane * group + peer}, device_id_type=MESH,
        )

    def along(src, dst, send, recv, to):
        return pltpu.make_async_remote_copy(
            src_ref=src, dst_ref=dst.at[plane],
            send_sem=send.at[to], recv_sem=recv.at[plane],
            device_id={"layer": to * group + place}, device_id_type=MESH,
        )

    def arrived(dst, send, recv, slot, source):
        pltpu.make_async_remote_copy(
            src_ref=dst.at[slot], dst_ref=dst.at[slot],
            send_sem=send.at[slot], recv_sem=recv.at[slot],
            device_id={"layer": source}, device_id_type=MESH,
        ).wait_recv()

    def scatter_all(*refs):
        for k in range(1, group):
            across(*refs, k).start()

    def scatter_sent(*refs):
        for k in range(1, group):
            across(*refs, k).wait_send()

    def arrived_all(dst, send, recv):
        for k in range(1, group):
            slot = lax.rem(place + k, group)
            arrived(dst, send, recv, slot, plane * group + slot)

    def along_all(low, high, *refs):
        def go(to, carry):
            along(*refs, to).start()
            return carry

        lax.fori_loop(low, high, go, 0)

    def along_sent(low, high, *refs):
        def go(to, carry):
            along(*refs, to).wait_send()
            return carry

        lax.fori_loop(low, high, go, 0)

    def compose(parts, comp, order):
        run = parts[order[0], :top]
        all_gain = fin[order[0], top : top + 1]
        for k in order[1:]:
            step = fin[k, top : top + 1]
            run = step * run + parts[k, :top]
            all_gain = step * all_gain
        comp[:top] = run
        comp[top:] = jnp.broadcast_to(all_gain, (8, 2 * ch))

    pack(field - lead * start, c, fsend)
    fsend[:, top:] = jnp.broadcast_to(gain_two[None], (group, 8, 2 * ch))
    scatter_all(fsend, fin, fs_send, fs_recv)

    end = cells_of(adj[...], c, ch)
    lam = end
    for d in reversed(range(depth_count)):
        act = acts[d]
        sens = step_size * (1.0 - act * act) * lam
        total = jnp.sum(sens, axis=0, keepdims=True)
        gbuf[mine, d, 3 * ch :, :] = jnp.broadcast_to(
            jnp.concatenate([total, total, total], axis=1), (8, 3 * ch)
        )
        s3 = jnp.concatenate([up(sens, c), sens, down(sens, c)], axis=1).astype(BF16)
        s3s[d] = s3
        t = lax.dot_general(s3, kf[d], (((1,), (1,)), ((), ())), preferred_element_type=F32)
        lam = (
            lam
            + t[:, ch : 2 * ch]
            + jnp.where(has_right, up(t[:, :ch], 1), 0.0)
            + jnp.where(has_left, down(t[:, 2 * ch :], 1), 0.0)
        )

    pack(lam - tail * end, c, asend)
    scatter_all(asend, ain, as_send, as_recv)

    fin[place] = fsend[place]
    ain[place] = asend[place]
    arrived_all(fin, fs_send, fs_recv)
    compose(fin, fcomp, range(group))
    along_all(plane + 1, planes, fcomp, fz, fz_send, fz_recv)
    arrived_all(ain, as_send, as_recv)
    compose(ain, acomp, range(group - 1, -1, -1))
    along_all(0, plane, acomp, az, az_send, az_recv)

    def pair(d, peer):
        return pltpu.make_async_remote_copy(
            src_ref=gbuf.at[mine, d], dst_ref=gbuf.at[mine, d],
            send_sem=g_send.at[peer, d], recv_sem=g_recv.at[mine, d],
            device_id={"dp": peer}, device_id_type=MESH,
        )

    def share(d):
        gbuf[mine, d, : 3 * ch, :] = lax.dot_general(
            xs[d], s3s[d], (((0,), (0,)), ((), ())), preferred_element_type=F32
        )

        def go(k, carry):
            pair(d, lax.rem(mine + k, m)).start()
            return carry

        lax.fori_loop(1, m, go, 0)

    for d in range(depth_count):
        share(d)

    def earlier(k, run):
        arrived(fz, fz_send, fz_recv, k, k * group + place)
        return fz[k, top : top + 1] * run + fz[k, :top]

    run = lax.fori_loop(0, plane, earlier, jnp.zeros((top, 2 * ch), F32))
    for k in range(group):
        fout[k] = run
        if k < group - 1:
            run = fin[k, top : top + 1] * run + fin[k, :top]
    fres[place] = fout[place]
    scatter_all(fout, fres, fr_send, fr_recv)

    def later(k, run):
        at = planes - 1 - k
        arrived(az, az_send, az_recv, at, at * group + place)
        return az[at, top : top + 1] * run + az[at, :top]

    run = lax.fori_loop(0, planes - 1 - plane, later, jnp.zeros((top, 2 * ch), F32))
    for k in range(group - 1, -1, -1):
        run = fin[k, top : top + 1] * run + ain[k]
        aout[k] = run
    ares[place] = aout[place]
    scatter_all(aout, ares, ar_send, ar_recv)

    arrived_all(fres, fr_send, fr_recv)

    @pl.when(me == 0)
    def _():
        out_s[...] = st[...]

    @pl.when(me > 0)
    def _():
        unpack(fres, out_s, c)

    for d in range(depth_count):

        def go(k, carry):
            source = lax.rem(mine + k, m)
            pltpu.make_async_remote_copy(
                src_ref=gbuf.at[source, d], dst_ref=gbuf.at[source, d],
                send_sem=g_send.at[source, d], recv_sem=g_recv.at[source, d],
                device_id={"dp": source}, device_id_type=MESH,
            ).wait_recv()
            return carry

        lax.fori_loop(1, m, go, 0)
        total = gbuf[0, d]
        for k in range(1, m):
            total = total + gbuf[k, d]
        total = total * (1.0 / images)
        for dy in range(3):
            for dx in range(3):
                out_k[d, dy, dx] = total[dy * ch : (dy + 1) * ch, dx * ch : (dx + 1) * ch]
        out_b[d : d + 1, :] = total[3 * ch : 3 * ch + 1, :ch]

    arrived_all(ares, ar_send, ar_recv)
    unpack(ares, out_a, c)

    scatter_sent(fsend, fin, fs_send, fs_recv)
    scatter_sent(asend, ain, as_send, as_recv)
    scatter_sent(fout, fres, fr_send, fr_recv)
    scatter_sent(aout, ares, ar_send, ar_recv)
    along_sent(plane + 1, planes, fcomp, fz, fz_send, fz_recv)
    along_sent(0, plane, acomp, az, az_send, az_recv)

    for d in range(depth_count):

        def gone(k, carry):
            pair(d, lax.rem(mine + k, m)).wait_send()
            return carry

        lax.fori_loop(1, m, gone, 0)


def body(states, adjoints, kernels, biases, coarse_gain):
    rows, flat = states.shape[2], states.shape[3]
    depth_count, ch = kernels.shape[0], kernels.shape[-1]
    cells = rows * flat // ch
    n, m = lax.axis_size("layer"), lax.axis_size("dp")
    images = m * states.shape[1]
    c = rows
    top = flat // (2 * ch) // group * rows
    planes = n // group
    vmem = pl.BlockSpec(memory_space=pltpu.VMEM)
    anywhere = pl.BlockSpec(memory_space=pl.ANY)
    hbm = pl.BlockSpec(memory_space=pltpu.HBM)
    wide = 2 * ch
    dma = pltpu.SemaphoreType.DMA
    results = pl.pallas_call(
        functools.partial(kernel, n, m, c, images),
        out_shape=(
            jax.ShapeDtypeStruct((rows, flat), F32),
            jax.ShapeDtypeStruct((rows, flat), F32),
            jax.ShapeDtypeStruct(kernels.shape, F32),
            jax.ShapeDtypeStruct(biases.shape, F32),
        ),
        in_specs=[vmem] * 3,
        out_specs=(vmem,) * 4,
        scratch_shapes=[
            pltpu.VMEM((depth_count, cells, 3 * ch), BF16),
            pltpu.VMEM((depth_count, cells, ch), F32),
            pltpu.VMEM((depth_count, cells, 3 * ch), BF16),
            pltpu.VMEM((depth_count, 3 * ch, 3 * ch), BF16),
            pltpu.VMEM((group, top + 8, wide), F32),
            pltpu.VMEM((group, top, wide), F32),
            pltpu.VMEM((group, top + 8, wide), F32),
            pltpu.VMEM((group, top, wide), F32),
            pltpu.VMEM((top + 8, wide), F32),
            pltpu.VMEM((top + 8, wide), F32),
            pltpu.VMEM((planes, top + 8, wide), F32),
            pltpu.VMEM((planes, top + 8, wide), F32),
            pltpu.VMEM((group, top, wide), F32),
            pltpu.VMEM((group, top, wide), F32),
            pltpu.VMEM((group, top, wide), F32),
            pltpu.VMEM((group, top, wide), F32),
            pltpu.VMEM((m, depth_count, 3 * ch + 8, 3 * ch), F32),
        ]
        + [dma((group,))] * 8
        + [dma((planes,))] * 4
        + [dma((m, depth_count))] * 2,
        compiler_params=pltpu.CompilerParams(
            collective_id=0, has_side_effects=True, vmem_limit_bytes=48 * 1024 * 1024
        ),
    )(
        jnp.concatenate([states[0, 0], adjoints[0, 0]]),
        kernels,
        jnp.concatenate([biases, coarse_gain]),
    )
    return pl.pallas_call(
        store,
        out_shape=(
            jax.ShapeDtypeStruct(states.shape, F32),
            jax.ShapeDtypeStruct(states.shape, F32),
            jax.ShapeDtypeStruct(kernels.shape, F32),
            jax.ShapeDtypeStruct(biases.shape, F32),
        ),
        in_specs=[anywhere] * 4,
        out_specs=(hbm,) * 4,
        scratch_shapes=[dma((4,))],
        compiler_params=pltpu.CompilerParams(vmem_limit_bytes=1024 * 1024),
    )(*results)


def solution(mesh):
    return jax.shard_map(
        body,
        mesh=mesh,
        in_specs=(
            P("layer", "dp", None, None),
            P("layer", "dp", None, None),
            P("layer", None, None, None, None),
            P("layer", None),
            P("layer", None),
        ),
        out_specs=(
            P("layer", "dp", None, None),
            P("layer", "dp", None, None),
            P("layer", None, None, None, None),
            P("layer", None),
        ),
        check_vma=False,
    )
```
